32 devices in a mesh: elem: 2 (over x), band: 16 (over z, y, core).
Axes of the slice: x: 2, y: 2, z: 4, core: 2. Of those that a mesh axis runs over, the one named last changes fastest.
Arguments:
- start_bands: bfloat16 [2048, 1536], P('band', 'elem'), may hold values from -6 to 6
- hamiltonian: bfloat16 [8, 7, 192, 192], P('elem'), may hold values from -0.15625 to 0.15625
- neighbours: int32 [8, 6], P('elem'), may hold values from 0 to 3
- basis_count: int32 [8], P('elem'), may hold values from 128 to 192, as said below
- owner_rows: int32 [16], replicated, may hold values from 1 to 144, 768 in all
- rotation: bfloat16 [2048, 2048], P(None, 'band'), may hold values from -0.125 to 0.125
Outputs:
- filtered: bfloat16 [2048, 1536], P('band', 'elem')
- rotated: bfloat16 [4608, 2048], P(('elem', 'band'))
The draws below stay inside these ranges and needn't reach their ends.
Inputs may be any that keep to these rules, and one draw needn't show every extreme that they name: `basis_count`: each element holds 128 to 192 basis functions; some element holds exactly 192 and some exactly 128. `neighbours`: any position 0 to 3 may appear in any slot, the element's own position too. `owner_rows`: the entries sum to 768; the largest is exactly 144.
All inputs are finite; a program needn't handle non-finite values.
Results may differ from the reference program's by a relative error of at most 0.013.
Values may be sent and summed in bfloat16 or wider, within the bound.
A program may use at most 64 MiB of HBM per device.

```python
import math
import jax
import jax.numpy as jnp
import numpy as np
from jax import lax

NB = 192
NBMIN = 128
BANDS = 2048
DEGREE = 8
GROUPS = 2
PLANES = 2
ELEMS = 8
ROWS = 1536
ROWS_GRP = 768
OWNERS = 16
CAP = 144


def draw_basis_count(key, part):
    key_counts, key_places = jax.random.split(jax.random.fold_in(key, 11))
    counts_drawn = jax.random.randint(key_counts, (ELEMS,), NBMIN, NB + 1, dtype=jnp.int32)
    positions = jax.random.permutation(key_places, ELEMS)
    counts_drawn = counts_drawn.at[positions[0]].set(NB)
    counts_drawn = counts_drawn.at[positions[1]].set(NBMIN)
    return counts_drawn


def with_ends(result, key, low, largest):
    place = [jax.random.randint(jax.random.fold_in(key, axis), (), 0, length) for axis, length in enumerate(result.shape)]
    main_axis = result.shape.index(max(result.shape))
    neighbour = place[:main_axis] + [(place[main_axis] + 1) % result.shape[main_axis]] + place[main_axis + 1:]
    return result.at[tuple(place)].set(low).at[tuple(neighbour)].set(largest)


def block_scale(own_key, extent, cuts, low, top_value):
    level, own = 1.0, jax.random.fold_in(own_key, 6)
    for position, blocks in cuts:
        heights = jnp.exp(jax.random.uniform(jax.random.fold_in(own, position), (blocks,), jnp.float32, low / len(cuts), top_value / len(cuts)))
        level = level * jnp.repeat(heights, extent[position] // blocks).reshape([-1 if axis == position else 1 for axis in range(len(extent))])
    return level


def split_up(number_of, total, limit, skew):
    weights = [(1 << 20) // math.isqrt(grade ** skew) + 1 for grade in range(2, number_of + 1)]
    spare, given = total - limit - (number_of - 1), [1] * (number_of - 1)
    while spare > 0:
        free = [i for i in range(number_of - 1) if given[i] < limit]
        pool, left = sum([weights[i] for i in free]), spare
        for i in free:
            more = min(limit - given[i], max(1, left * weights[i] // pool), spare)
            given[i] = given[i] + more
            spare = spare - more
    return np.array([limit] + given)


def ragged_sizes(stream_key, amount, total, most, skew):
    if amount == 2:
        one = jax.random.randint(stream_key, (), max(1, total - most), min(most, total - 1) + 1)
        return jnp.stack([one, total - one])
    tallies = jnp.asarray(split_up(amount, total, most, skew), jnp.int32)
    pairs = (amount - 1) // 2
    donor, taker = tallies[1:1 + 2 * pairs:2], tallies[2:2 + 2 * pairs:2]
    room = jnp.minimum(donor - 1, most - taker)
    passed = jax.random.randint(jax.random.fold_in(stream_key, 1), (pairs,), 0, 1 << 20) % (room + 1)
    tallies = tallies.at[1:1 + 2 * pairs:2].set(donor - passed).at[2:2 + 2 * pairs:2].set(taker + passed)
    return tallies[jax.random.permutation(jax.random.fold_in(stream_key, 2), amount)]


def noise(key, dims, width, limit, cuts=(), held_as=jnp.bfloat16):
    gain = block_scale(key, dims, cuts, -0.22, 0.18) if cuts else 1.0
    values = jax.random.normal(key, dims, jnp.float32) * width * gain
    return jnp.minimum(jnp.maximum(values, -limit), limit).astype(held_as)


def setup_inputs(seed: int = 0) -> dict:
    key_list = jax.random.split(jax.random.key(seed), 7)
    return {
        "start_bands": noise(key_list[0], (BANDS, ROWS), 1.0, 6.0, ((0, 16), (1, 2))),
        "hamiltonian": noise(key_list[1], (ELEMS, 7, NB, NB), (7 * NB) ** -0.5, 0.15625, ((0, 2),)),
        "neighbours": with_ends(jax.random.randint(key_list[2], (ELEMS, 6), 0, 4), jax.random.fold_in(key_list[2], 1), 0, 3).astype(jnp.int32),
        "basis_count": draw_basis_count(jax.random.fold_in(key_list[6], 71), 0),
        "owner_rows": ragged_sizes(key_list[4], OWNERS, ROWS_GRP, CAP, 2).astype(jnp.int32),
        "rotation": noise(key_list[5], (BANDS, BANDS), BANDS ** -0.5, 0.125, ((1, 16),)),
    }


def apply_ham(state, blocks_f32, partner_grid, row_mask):
    state_grid = state.reshape(BANDS, PLANES, 4, NB)

    def plane_apply(plane):
        below = jnp.take(state_grid, (plane + PLANES - 1) % PLANES, axis=1)
        middle = jnp.take(state_grid, plane, axis=1)
        above = jnp.take(state_grid, (plane + 1) % PLANES, axis=1)
        partner = jnp.take(partner_grid, plane, axis=0)
        columns = [middle]
        for slot_no in range(4):
            columns.append(middle[:, partner[:, slot_no]])
        columns.append(below[:, partner[:, 4]])
        columns.append(above[:, partner[:, 5]])
        sources = jnp.stack(columns, axis=2).reshape(BANDS, 4, 7 * NB).astype(jnp.float32)
        plane_blocks = jnp.take(blocks_f32, plane, axis=0)
        return jnp.einsum("bij,ijl->ibl", sources, plane_blocks, precision=lax.Precision.HIGHEST,
                          preferred_element_type=jnp.float32)

    stacked = lax.map(plane_apply, jnp.arange(PLANES, dtype=jnp.int32))
    return stacked.transpose(2, 0, 1, 3).reshape(BANDS, ROWS) * row_mask


def reference(start_bands, hamiltonian, neighbours, basis_count, owner_rows, rotation):
    basis_ids = lax.broadcasted_iota(jnp.int32, (ELEMS, NB), 1)
    row_mask = (basis_ids < basis_count[:, None]).astype(jnp.float32).reshape(ROWS)
    blocks_f32 = hamiltonian.reshape(PLANES, 4, 7 * NB, NB).astype(jnp.float32)
    partner_grid = neighbours.reshape(PLANES, 4, 6)
    earlier = (start_bands.astype(jnp.float32) * row_mask).astype(jnp.bfloat16)
    current = (0.5 * apply_ham(earlier, blocks_f32, partner_grid, row_mask)).astype(jnp.bfloat16)
    for repeat in range(DEGREE - 1):
        following = (apply_ham(current, blocks_f32, partner_grid, row_mask) - earlier.astype(jnp.float32)).astype(jnp.bfloat16)
        earlier = current
        current = following
    filtered = current
    turned = jnp.dot(filtered.T, rotation, preferred_element_type=jnp.float32).astype(jnp.bfloat16)
    row_start = (jnp.cumsum(owner_rows) - owner_rows).astype(jnp.int32)
    slot_ids = jnp.arange(CAP, dtype=jnp.int32)
    group_ids = jnp.arange(GROUPS, dtype=jnp.int32)
    row_index = group_ids[:, None, None] * ROWS_GRP + row_start[None, :, None] + slot_ids[None, None, :]
    slot_keep = jnp.broadcast_to((slot_ids[None, :] < owner_rows[:, None])[None], row_index.shape).reshape(-1)
    picked = jnp.take(turned, jnp.minimum(row_index, ROWS - 1).reshape(-1).astype(jnp.int32), axis=0)
    rotated = jnp.where(slot_keep[:, None], picked, jnp.zeros((), jnp.bfloat16))
    return filtered, rotated
```

```python
import functools

import jax
import jax.numpy as jnp
from jax import lax
from jax.experimental import pallas as pl
from jax.experimental.pallas import tpu as pltpu
from jax.sharding import PartitionSpec as P

DEGREE = 8


def padded_2(block, sides, width):
    for axis, dim in sides:
        count = lax.axis_size(axis)
        forward = [(i, i + 1) for i in range(count - 1)]
        forward.append((count - 1, 0))
        backward = [(target, source) for source, target in forward]
        low = lax.ppermute(
            lax.slice_in_dim(block, block.shape[dim] - width, None, axis=dim), axis, forward
        )
        high = lax.ppermute(lax.slice_in_dim(block, 0, width, axis=dim), axis, backward)
        block = jnp.concatenate([low, block, high], axis=dim)
    return block


def per_device(start_bands, hamiltonian, neighbours, basis_count, owner_rows, rotation):
    bands_dev, rows_dev = start_bands.shape
    elem_count = hamiltonian.shape[0]
    basis_max = hamiltonian.shape[2]
    planes_dev = elem_count // 4
    basis_ids = lax.broadcasted_iota(jnp.int32, (elem_count, basis_max), 1)
    row_mask = (basis_ids < basis_count[:, None]).astype(jnp.float32).reshape(rows_dev)
    partner_pick = (neighbours[:, :, None] == jnp.arange(4, dtype=jnp.int32)[None, None, :]).astype(
        jnp.bfloat16
    )
    partner_pick = partner_pick.reshape(planes_dev, 4, 6, 4)
    weights = hamiltonian.reshape(elem_count, 7 * basis_max, basis_max)

    def apply_ham(state):
        plane_slab = state.reshape(bands_dev, planes_dev, 4 * basis_max)
        extended = padded_2(plane_slab, (("elem", 1),), 1)
        extended = extended.reshape(bands_dev, planes_dev + 2, 4, basis_max)
        plane_below = extended[:, :planes_dev]
        plane_mid = extended[:, 1 : planes_dev + 1]
        plane_above = extended[:, 2:]
        inplane = jnp.einsum(
            "pism,bpmk->bpisk",
            partner_pick[:, :, :4],
            plane_mid,
            preferred_element_type=jnp.float32,
        ).astype(jnp.bfloat16)
        lower = jnp.einsum(
            "pim,bpmk->bpik", partner_pick[:, :, 4], plane_below, preferred_element_type=jnp.float32
        ).astype(jnp.bfloat16)
        upper = jnp.einsum(
            "pim,bpmk->bpik", partner_pick[:, :, 5], plane_above, preferred_element_type=jnp.float32
        ).astype(jnp.bfloat16)
        sources = jnp.concatenate(
            [plane_mid[:, :, :, None], inplane, lower[:, :, :, None], upper[:, :, :, None]], axis=3
        )
        sources = sources.reshape(bands_dev, elem_count, 7 * basis_max)
        product = jnp.einsum("bej,ejl->bel", sources, weights, preferred_element_type=jnp.float32)
        return product.reshape(bands_dev, rows_dev) * row_mask

    earlier = (start_bands.astype(jnp.float32) * row_mask).astype(jnp.bfloat16)
    current = (0.5 * apply_ham(earlier)).astype(jnp.bfloat16)
    for repeat in range(DEGREE - 1):
        following = (apply_ham(current) - earlier.astype(jnp.float32)).astype(jnp.bfloat16)
        earlier = current
        current = following
    owners = lax.axis_size("band")
    slot_cap = 3 * rows_dev // owners
    before = jnp.arange(owners)[None, :] < jnp.arange(owners)[:, None]
    row_starts = jnp.sum(jnp.where(before, owner_rows[None, :], 0), axis=1)
    slot_keep = jnp.arange(slot_cap, dtype=jnp.int32)[None, :] < owner_rows[:, None]
    padded = jnp.concatenate([current, jnp.zeros((bands_dev, slot_cap), jnp.bfloat16)], axis=1)
    pieces = jax.vmap(lambda offset: lax.dynamic_slice_in_dim(padded, offset, slot_cap, 1))(
        row_starts
    )
    owned_rows = lax.all_to_all(
        jnp.where(slot_keep[:, None, :], pieces, jnp.zeros((), jnp.bfloat16)),
        "band",
        split_axis=0,
        concat_axis=1,
        tiled=True,
    ).reshape(-1, slot_cap)
    rotated = lax.dot_general(
        owned_rows,
        lax.all_gather(rotation, "band", axis=1, tiled=True),
        (((0,), (0,)), ((), ())),
        preferred_element_type=jnp.float32,
    ).astype(jnp.bfloat16)
    return (current, rotated)


def filter_kernel(
    owners,
    start_ref,
    ham_ref,
    nb_ref,
    count_ref,
    owner_ref,
    filtered_ref,
    owned_ref,
    amat,
    bands,
    masked,
    swapped,
    pieces,
    arrived,
    band_send,
    band_recv,
    strip_send,
    strip_recv,
    core_send,
    core_recv,
    back_send,
    back_recv,
    piece_send,
    piece_recv,
):
    e = lax.axis_index("elem")
    b = lax.axis_index("band")
    o = 1 - e
    core = lax.rem(b, 2)
    sib = b + 1 - 2 * core
    count, rows = start_ref.shape
    half = count // 2
    nb = ham_ref.shape[2]
    cap = owned_ref.shape[0]

    barrier = pltpu.get_barrier_semaphore()
    pl.semaphore_signal(barrier, inc=1, device_id={"elem": o}, device_id_type=pl.DeviceIdType.MESH)

    def greet(d, carry):
        j = lax.rem(b + d, owners)
        pl.semaphore_signal(
            barrier, inc=1, device_id={"band": j}, device_id_type=pl.DeviceIdType.MESH
        )
        return carry

    lax.fori_loop(1, owners, greet, 0)
    pl.semaphore_wait(barrier, owners)

    lane = lax.broadcasted_iota(jnp.int32, (1, rows), 1)
    keep = jnp.zeros((1, rows), jnp.float32)
    for i in range(4):
        inside = (lane >= nb * i) & (lane < nb * i + count_ref[i])
        keep = jnp.where(inside, 1.0, keep)
    masked[...] = (start_ref[...].astype(jnp.float32) * keep).astype(jnp.bfloat16)
    own_cols = pl.ds(pl.multiple_of(rows * e, 128), rows)
    other_cols = pl.ds(pl.multiple_of(rows * o, 128), rows)
    own_half = pl.ds(pl.multiple_of(half * e, 16), half)
    other_half = pl.ds(pl.multiple_of(half * o, 16), half)
    band_copy = pltpu.make_async_remote_copy(
        src_ref=masked.at[other_half],
        dst_ref=bands.at[0, :, own_cols],
        send_sem=band_send,
        recv_sem=band_recv,
        device_id={"elem": o},
        device_id_type=pl.DeviceIdType.MESH,
    )
    band_copy.start()
    bands[0, :, own_cols] = masked[own_half, :]

    def strip_rows(step, side):
        t = 4 * side + step
        return pl.ds(pl.multiple_of(t * nb, 16), nb)

    def build(step, side):
        t = 4 * side + step
        parts = []
        for i in range(4):
            total = jnp.where(t == 4 * e + i, 1.0, 0.0) * ham_ref[i, 0].astype(jnp.float32)
            for j in range(1, 7):
                plane = e if j < 5 else o
                pick = jnp.where(nb_ref[i, j - 1] + 4 * plane == t, 1.0, 0.0)
                total = total + pick * ham_ref[i, j].astype(jnp.float32)
            parts.append(total)
        strip = jnp.concatenate(parts, axis=1) * keep
        amat[e, strip_rows(step, side), :] = strip.astype(jnp.bfloat16)

    def to_partner(step):
        where = strip_rows(step, core)
        return pltpu.make_async_remote_copy(
            src_ref=amat.at[e, where],
            dst_ref=amat.at[e, where],
            send_sem=strip_send.at[step],
            recv_sem=strip_recv.at[step],
            device_id={"elem": o},
            device_id_type=pl.DeviceIdType.MESH,
        )

    def from_partner(step):
        where = strip_rows(step, core)
        return pltpu.make_async_remote_copy(
            src_ref=amat.at[o, where],
            dst_ref=amat.at[o, where],
            send_sem=strip_send.at[step],
            recv_sem=strip_recv.at[step],
            device_id={"elem": o},
            device_id_type=pl.DeviceIdType.MESH,
        )

    def to_sibling(step, side):
        where = strip_rows(step, side)
        return pltpu.make_async_remote_copy(
            src_ref=amat.at[o, where],
            dst_ref=amat.at[o, where],
            send_sem=core_send.at[step],
            recv_sem=core_recv.at[step],
            device_id={"band": sib},
            device_id_type=pl.DeviceIdType.MESH,
        )

    def first_half(step, carry):
        build(step, core)
        to_partner(step).start()
        return carry

    def second_half(step, carry):
        build(step, 1 - core)
        return carry

    def forward(step, carry):
        from_partner(step).wait_recv()
        to_sibling(step, core).start()
        return carry

    def collect(step, carry):
        to_sibling(step, 1 - core).wait_recv()
        to_sibling(step, core).wait_send()
        to_partner(step).wait_send()
        return carry

    lax.fori_loop(0, 4, first_half, 0)
    lax.fori_loop(0, 4, second_half, 0)
    lax.fori_loop(0, 4, forward, 0)
    lax.fori_loop(0, 4, collect, 0)
    band_copy.wait_send()
    pltpu.make_async_remote_copy(
        src_ref=masked.at[other_half],
        dst_ref=bands.at[0, :, other_cols],
        send_sem=band_send,
        recv_sem=band_recv,
        device_id={"elem": o},
        device_id_type=pl.DeviceIdType.MESH,
    ).wait_recv()

    wide = 256 if rows % 256 == 0 else rows

    def advance(now, later, first):
        for p in range(2):
            for c in range(rows // wide):
                product = jnp.dot(
                    bands[now],
                    amat[p, :, c * wide : (c + 1) * wide],
                    preferred_element_type=jnp.float32,
                )
                cols = slice(p * rows + c * wide, p * rows + (c + 1) * wide)
                if first:
                    product = 0.5 * product
                else:
                    product = product - bands[later, :, cols].astype(jnp.float32)
                bands[later, :, cols] = product.astype(jnp.bfloat16)

    advance(0, 1, True)

    def two_steps(k, carry):
        advance(1, 0, False)
        advance(0, 1, False)
        return carry

    lax.fori_loop(0, (DEGREE - 2) // 2, two_steps, 0)
    advance(1, 0, False)

    back = pltpu.make_async_remote_copy(
        src_ref=bands.at[0, :, other_cols],
        dst_ref=swapped,
        send_sem=back_send,
        recv_sem=back_recv,
        device_id={"elem": o},
        device_id_type=pl.DeviceIdType.MESH,
    )
    back.start()
    masked[own_half, :] = bands[0, :, own_cols]
    back.wait()
    masked[other_half, :] = swapped[...]
    filtered_ref[...] = masked[...]

    lanes = lax.broadcasted_iota(jnp.int32, (cap, rows), 1)
    slots = lax.broadcasted_iota(jnp.int32, (cap, rows), 0)

    def piece(j):
        begin = jnp.int32(0)
        for i in range(owners):
            begin = begin + jnp.where(i < j, owner_ref[i], 0)
        chosen = (lanes == slots + begin) & (slots < owner_ref[j])
        pick = jnp.where(chosen, 1.0, 0.0).astype(jnp.bfloat16)
        return lax.dot_general(
            pick, masked[...], (((1,), (1,)), ((), ())), preferred_element_type=jnp.float32
        ).astype(jnp.bfloat16)

    def piece_copy(j, origin):
        return pltpu.make_async_remote_copy(
            src_ref=pieces.at[j],
            dst_ref=arrived.at[origin],
            send_sem=piece_send.at[j],
            recv_sem=piece_recv.at[origin],
            device_id={"band": j},
            device_id_type=pl.DeviceIdType.MESH,
        )

    def send(d, carry):
        j = lax.rem(b + d, owners)
        pieces[j] = piece(j)
        piece_copy(j, b).start()
        return carry

    lax.fori_loop(1, owners, send, 0)
    arrived[b] = piece(b)

    def receive(d, carry):
        j = lax.rem(b + d, owners)
        piece_copy(j, j).wait_recv()
        piece_copy(j, b).wait_send()
        return carry

    lax.fori_loop(1, owners, receive, 0)
    for i in range(owners):
        owned_ref[:, i * count : (i + 1) * count] = arrived[i]


def turn_kernel(owned_ref, rotation_ref, out_ref):
    wide = jnp.concatenate([rotation_ref[0], rotation_ref[1]], axis=1)
    out_ref[...] = jnp.dot(
        owned_ref[...], wide, preferred_element_type=jnp.float32
    ).astype(jnp.bfloat16)


def per_device_pair(start_bands, hamiltonian, neighbours, basis_count, owner_rows, rotation):
    bands_dev, rows_dev = start_bands.shape
    owners = lax.axis_size("band")
    cap = 3 * rows_dev // owners
    bands_all, width = rotation.shape
    nb = hamiltonian.shape[2]
    gathered = lax.all_gather(rotation, "band", axis=0, tiled=False)
    vmem = pl.BlockSpec(memory_space=pltpu.VMEM)
    smem = pl.BlockSpec(memory_space=pltpu.SMEM)
    dma = pltpu.SemaphoreType.DMA
    bf16 = jnp.bfloat16
    filtered, owned = pl.pallas_call(
        functools.partial(filter_kernel, owners),
        out_shape=(
            jax.ShapeDtypeStruct((bands_dev, rows_dev), bf16),
            jax.ShapeDtypeStruct((cap, bands_all), bf16),
        ),
        in_specs=[vmem, vmem, smem, smem, smem],
        out_specs=(vmem, vmem),
        scratch_shapes=[
            pltpu.VMEM((2, 2 * rows_dev, rows_dev), bf16),
            pltpu.VMEM((2, bands_dev // 2, 2 * rows_dev), bf16),
            pltpu.VMEM((bands_dev, rows_dev), bf16),
            pltpu.VMEM((bands_dev // 2, rows_dev), bf16),
            pltpu.VMEM((owners, cap, bands_dev), bf16),
            pltpu.VMEM((owners, cap, bands_dev), bf16),
            dma,
            dma,
            dma((4,)),
            dma((4,)),
            dma((4,)),
            dma((4,)),
            dma,
            dma,
            dma((owners,)),
            dma((owners,)),
        ],
        compiler_params=pltpu.CompilerParams(
            collective_id=0, has_side_effects=True, vmem_limit_bytes=40 * 1024 * 1024
        ),
        cost_estimate=pl.CostEstimate(
            flops=16 * bands_dev * 2 * rows_dev * rows_dev,
            bytes_accessed=200_000_000,
            transcendentals=0,
        ),
    )(start_bands, hamiltonian, neighbours, basis_count, owner_rows)
    rotated = pl.pallas_call(
        turn_kernel,
        grid=(owners // 2,),
        out_shape=jax.ShapeDtypeStruct((cap, owners * width), bf16),
        in_specs=[
            pl.BlockSpec((cap, bands_all), lambda s: (0, 0)),
            pl.BlockSpec((2, bands_all, width), lambda s: (s, 0, 0)),
        ],
        out_specs=pl.BlockSpec((cap, 2 * width), lambda s: (0, s)),
        compiler_params=pltpu.CompilerParams(vmem_limit_bytes=24 * 1024 * 1024),
    )(owned, gathered)
    return filtered, rotated


def solution(mesh):
    pair = mesh.shape["elem"] == 2 and mesh.shape["band"] % 2 == 0
    placed = (
        P("band", "elem"),
        P("elem", None, None, None),
        P("elem", None),
        P("elem"),
        P(),
        P(None, "band"),
    )
    return jax.shard_map(
        per_device_pair if pair else per_device,
        mesh=mesh,
        in_specs=placed,
        out_specs=(P("band", "elem"), P(("elem", "band"), None)),
        check_vma=False,
    )
```

```python
import functools

import jax
import jax.numpy as jnp
from jax import lax
from jax.experimental import pallas as pl
from jax.experimental.pallas import tpu as pltpu
from jax.sharding import PartitionSpec as P

DEGREE = 8


def padded_2(block, sides, width):
    for axis, dim in sides:
        count = lax.axis_size(axis)
        forward = [(i, i + 1) for i in range(count - 1)]
        forward.append((count - 1, 0))
        backward = [(target, source) for source, target in forward]
        low = lax.ppermute(
            lax.slice_in_dim(block, block.shape[dim] - width, None, axis=dim), axis, forward
        )
        high = lax.ppermute(lax.slice_in_dim(block, 0, width, axis=dim), axis, backward)
        block = jnp.concatenate([low, block, high], axis=dim)
    return block


def per_device(start_bands, hamiltonian, neighbours, basis_count, owner_rows, rotation):
    bands_dev, rows_dev = start_bands.shape
    elem_count = hamiltonian.shape[0]
    basis_max = hamiltonian.shape[2]
    planes_dev = elem_count // 4
    basis_ids = lax.broadcasted_iota(jnp.int32, (elem_count, basis_max), 1)
    row_mask = (basis_ids < basis_count[:, None]).astype(jnp.float32).reshape(rows_dev)
    partner_pick = (neighbours[:, :, None] == jnp.arange(4, dtype=jnp.int32)[None, None, :]).astype(
        jnp.bfloat16
    )
    partner_pick = partner_pick.reshape(planes_dev, 4, 6, 4)
    weights = hamiltonian.reshape(elem_count, 7 * basis_max, basis_max)

    def apply_ham(state):
        plane_slab = state.reshape(bands_dev, planes_dev, 4 * basis_max)
        extended = padded_2(plane_slab, (("elem", 1),), 1)
        extended = extended.reshape(bands_dev, planes_dev + 2, 4, basis_max)
        plane_below = extended[:, :planes_dev]
        plane_mid = extended[:, 1 : planes_dev + 1]
        plane_above = extended[:, 2:]
        inplane = jnp.einsum(
            "pism,bpmk->bpisk",
            partner_pick[:, :, :4],
            plane_mid,
            preferred_element_type=jnp.float32,
        ).astype(jnp.bfloat16)
        lower = jnp.einsum(
            "pim,bpmk->bpik", partner_pick[:, :, 4], plane_below, preferred_element_type=jnp.float32
        ).astype(jnp.bfloat16)
        upper = jnp.einsum(
            "pim,bpmk->bpik", partner_pick[:, :, 5], plane_above, preferred_element_type=jnp.float32
        ).astype(jnp.bfloat16)
        sources = jnp.concatenate(
            [plane_mid[:, :, :, None], inplane, lower[:, :, :, None], upper[:, :, :, None]], axis=3
        )
        sources = sources.reshape(bands_dev, elem_count, 7 * basis_max)
        product = jnp.einsum("bej,ejl->bel", sources, weights, preferred_element_type=jnp.float32)
        return product.reshape(bands_dev, rows_dev) * row_mask

    earlier = (start_bands.astype(jnp.float32) * row_mask).astype(jnp.bfloat16)
    current = (0.5 * apply_ham(earlier)).astype(jnp.bfloat16)
    for repeat in range(DEGREE - 1):
        following = (apply_ham(current) - earlier.astype(jnp.float32)).astype(jnp.bfloat16)
        earlier = current
        current = following
    owners = lax.axis_size("band")
    slot_cap = 3 * rows_dev // owners
    before = jnp.arange(owners)[None, :] < jnp.arange(owners)[:, None]
    row_starts = jnp.sum(jnp.where(before, owner_rows[None, :], 0), axis=1)
    slot_keep = jnp.arange(slot_cap, dtype=jnp.int32)[None, :] < owner_rows[:, None]
    padded = jnp.concatenate([current, jnp.zeros((bands_dev, slot_cap), jnp.bfloat16)], axis=1)
    pieces = jax.vmap(lambda offset: lax.dynamic_slice_in_dim(padded, offset, slot_cap, 1))(
        row_starts
    )
    owned_rows = lax.all_to_all(
        jnp.where(slot_keep[:, None, :], pieces, jnp.zeros((), jnp.bfloat16)),
        "band",
        split_axis=0,
        concat_axis=1,
        tiled=True,
    ).reshape(-1, slot_cap)
    rotated = lax.dot_general(
        owned_rows,
        lax.all_gather(rotation, "band", axis=1, tiled=True),
        (((0,), (0,)), ((), ())),
        preferred_element_type=jnp.float32,
    ).astype(jnp.bfloat16)
    return (current, rotated)


def filter_kernel(
    owners,
    start_ref,
    ham_ref,
    nb_ref,
    count_ref,
    owner_ref,
    rotation_ref,
    filtered_ref,
    rotated_ref,
    owned_ref,
    columns,
    amat,
    bands,
    masked,
    swapped,
    pieces,
    arrived,
    band_send,
    band_recv,
    strip_send,
    strip_recv,
    core_send,
    core_recv,
    back_send,
    back_recv,
    piece_send,
    piece_recv,
    ring_send,
    ring_recv,
    share_send,
    share_recv,
    mine_send,
    mine_recv,
):
    e = lax.axis_index("elem")
    b = lax.axis_index("band")
    o = 1 - e
    core = lax.rem(b, 2)
    sib = b + 1 - 2 * core
    count, rows = start_ref.shape
    half = count // 2
    nb = ham_ref.shape[2]
    cap = owned_ref.shape[0]

    barrier = pltpu.get_barrier_semaphore()
    pl.semaphore_signal(barrier, inc=1, device_id={"elem": o}, device_id_type=pl.DeviceIdType.MESH)

    def greet(d, carry):
        j = lax.rem(b + d, owners)
        pl.semaphore_signal(
            barrier, inc=1, device_id={"band": j}, device_id_type=pl.DeviceIdType.MESH
        )
        return carry

    lax.fori_loop(1, owners, greet, 0)
    pl.semaphore_wait(barrier, owners)

    chips = owners // 2
    tall = chips // 2
    chip = b // 2
    layer = chip // 2
    place = jnp.where(lax.rem(chip, 2) == 0, layer, chips - 1 - layer)
    depth = rotation_ref.shape[0] // 2

    def member(position, which):
        position = lax.rem(position + 2 * chips, chips)
        near = 4 * position
        far = 4 * (chips - 1 - position) + 2
        return jnp.where(position < tall, near, far) + which

    def part(chunk, way):
        return columns.at[chunk, pl.ds(way * depth, depth)]

    def ring_copy(step, way, chunk):
        return pltpu.make_async_remote_copy(
            src_ref=part(chunk, way),
            dst_ref=part(chunk, way),
            send_sem=ring_send.at[way, step],
            recv_sem=ring_recv.at[way, step],
            device_id={"band": member(place + 1 - 2 * way, core)},
            device_id_type=pl.DeviceIdType.MESH,
        )

    def sent_chunk(step, way, which):
        return member(place - step + 2 * step * way, which)

    def share_copy(step, way, which):
        chunk = sent_chunk(step + 1, way, which)
        return pltpu.make_async_remote_copy(
            src_ref=part(chunk, way),
            dst_ref=part(chunk, way),
            send_sem=share_send.at[way, step],
            recv_sem=share_recv.at[way, step],
            device_id={"band": sib},
            device_id_type=pl.DeviceIdType.MESH,
        )

    def mine_copy(chunk):
        return pltpu.make_async_remote_copy(
            src_ref=columns.at[chunk],
            dst_ref=columns.at[chunk],
            send_sem=mine_send,
            recv_sem=mine_recv,
            device_id={"band": sib},
            device_id_type=pl.DeviceIdType.MESH,
        )

    def ring(step):
        for way in range(2):
            if step > 0:
                ring_copy(step - 1, way, sent_chunk(step, way, core)).wait_recv()
            if step < chips - 1:
                ring_copy(step, way, sent_chunk(step, way, core)).start()
            if step > 0:
                share_copy(step - 1, way, core).start()

    columns[b] = rotation_ref[...]
    ring(0)
    mine_copy(b).start()

    lane = lax.broadcasted_iota(jnp.int32, (1, rows), 1)
    keep = jnp.zeros((1, rows), jnp.float32)
    for i in range(4):
        inside = (lane >= nb * i) & (lane < nb * i + count_ref[i])
        keep = jnp.where(inside, 1.0, keep)
    masked[...] = (start_ref[...].astype(jnp.float32) * keep).astype(jnp.bfloat16)
    own_cols = pl.ds(pl.multiple_of(rows * e, 128), rows)
    other_cols = pl.ds(pl.multiple_of(rows * o, 128), rows)
    own_half = pl.ds(pl.multiple_of(half * e, 16), half)
    other_half = pl.ds(pl.multiple_of(half * o, 16), half)
    band_copy = pltpu.make_async_remote_copy(
        src_ref=masked.at[other_half],
        dst_ref=bands.at[0, :, own_cols],
        send_sem=band_send,
        recv_sem=band_recv,
        device_id={"elem": o},
        device_id_type=pl.DeviceIdType.MESH,
    )
    band_copy.start()
    bands[0, :, own_cols] = masked[own_half, :]

    def strip_rows(step, side):
        t = 4 * side + step
        return pl.ds(pl.multiple_of(t * nb, 16), nb)

    def build(step, side):
        t = 4 * side + step
        parts = []
        for i in range(4):
            total = jnp.where(t == 4 * e + i, 1.0, 0.0) * ham_ref[i, 0].astype(jnp.float32)
            for j in range(1, 7):
                plane = e if j < 5 else o
                pick = jnp.where(nb_ref[i, j - 1] + 4 * plane == t, 1.0, 0.0)
                total = total + pick * ham_ref[i, j].astype(jnp.float32)
            parts.append(total)
        strip = jnp.concatenate(parts, axis=1) * keep
        amat[e, strip_rows(step, side), :] = strip.astype(jnp.bfloat16)

    def to_partner(step):
        where = strip_rows(step, core)
        return pltpu.make_async_remote_copy(
            src_ref=amat.at[e, where],
            dst_ref=amat.at[e, where],
            send_sem=strip_send.at[step],
            recv_sem=strip_recv.at[step],
            device_id={"elem": o},
            device_id_type=pl.DeviceIdType.MESH,
        )

    def from_partner(step):
        where = strip_rows(step, core)
        return pltpu.make_async_remote_copy(
            src_ref=amat.at[o, where],
            dst_ref=amat.at[o, where],
            send_sem=strip_send.at[step],
            recv_sem=strip_recv.at[step],
            device_id={"elem": o},
            device_id_type=pl.DeviceIdType.MESH,
        )

    def to_sibling(step, side):
        where = strip_rows(step, side)
        return pltpu.make_async_remote_copy(
            src_ref=amat.at[o, where],
            dst_ref=amat.at[o, where],
            send_sem=core_send.at[step],
            recv_sem=core_recv.at[step],
            device_id={"band": sib},
            device_id_type=pl.DeviceIdType.MESH,
        )

    def first_half(step, carry):
        build(step, core)
        to_partner(step).start()
        return carry

    def second_half(step, carry):
        build(step, 1 - core)
        return carry

    def forward(step, carry):
        from_partner(step).wait_recv()
        to_sibling(step, core).start()
        return carry

    def collect(step, carry):
        to_sibling(step, 1 - core).wait_recv()
        to_sibling(step, core).wait_send()
        to_partner(step).wait_send()
        return carry

    lax.fori_loop(0, 4, first_half, 0)
    lax.fori_loop(0, 4, second_half, 0)
    early = max(chips - 3, 0)
    for step in range(4):
        if step + 1 <= early:
            ring(step + 1)
        forward(step, 0)
    for step in range(5, early + 1):
        ring(step)
    lax.fori_loop(0, 4, collect, 0)
    band_copy.wait_send()
    pltpu.make_async_remote_copy(
        src_ref=masked.at[other_half],
        dst_ref=bands.at[0, :, other_cols],
        send_sem=band_send,
        recv_sem=band_recv,
        device_id={"elem": o},
        device_id_type=pl.DeviceIdType.MESH,
    ).wait_recv()

    wide = 256 if rows % 256 == 0 else rows

    def advance(now, later, first):
        for p in range(2):
            for c in range(rows // wide):
                product = jnp.dot(
                    bands[now],
                    amat[p, :, c * wide : (c + 1) * wide],
                    preferred_element_type=jnp.float32,
                )
                cols = slice(p * rows + c * wide, p * rows + (c + 1) * wide)
                if first:
                    product = 0.5 * product
                else:
                    product = product - bands[later, :, cols].astype(jnp.float32)
                bands[later, :, cols] = product.astype(jnp.bfloat16)

    advance(0, 1, True)

    def two_steps(k, carry):
        advance(1, 0, False)
        advance(0, 1, False)
        return carry

    lax.fori_loop(0, (DEGREE - 2) // 2, two_steps, 0)
    advance(1, 0, False)

    back = pltpu.make_async_remote_copy(
        src_ref=bands.at[0, :, other_cols],
        dst_ref=swapped,
        send_sem=back_send,
        recv_sem=back_recv,
        device_id={"elem": o},
        device_id_type=pl.DeviceIdType.MESH,
    )
    back.start()
    for step in range(early + 1, chips - 1):
        ring(step)
    masked[own_half, :] = bands[0, :, own_cols]
    back.wait()
    masked[other_half, :] = swapped[...]
    filtered_ref[...] = masked[...]

    lanes = lax.broadcasted_iota(jnp.int32, (cap, rows), 1)
    slots = lax.broadcasted_iota(jnp.int32, (cap, rows), 0)

    def piece(j):
        begin = jnp.int32(0)
        for i in range(owners):
            begin = begin + jnp.where(i < j, owner_ref[i], 0)
        chosen = (lanes == slots + begin) & (slots < owner_ref[j])
        pick = jnp.where(chosen, 1.0, 0.0).astype(jnp.bfloat16)
        return lax.dot_general(
            pick, masked[...], (((1,), (1,)), ((), ())), preferred_element_type=jnp.float32
        ).astype(jnp.bfloat16)

    def piece_copy(j, origin):
        return pltpu.make_async_remote_copy(
            src_ref=pieces.at[j],
            dst_ref=arrived.at[origin],
            send_sem=piece_send.at[j],
            recv_sem=piece_recv.at[origin],
            device_id={"band": j},
            device_id_type=pl.DeviceIdType.MESH,
        )

    def send(d, carry):
        j = lax.rem(b + d, owners)
        pieces[j] = piece(j)
        piece_copy(j, b).start()
        return carry

    lax.fori_loop(1, owners, send, 0)
    arrived[b] = piece(b)

    def receive(d, carry):
        j = lax.rem(b + d, owners)
        piece_copy(j, j).wait_recv()
        piece_copy(j, b).wait_send()
        return carry

    ring(chips - 1)
    lax.fori_loop(1, owners, receive, 0)
    for i in range(owners):
        owned_ref[:, i * count : (i + 1) * count] = arrived[i]
    mine_copy(b).wait_send()
    mine_copy(sib).wait_recv()
    for step in range(chips - 1):
        for way in range(2):
            ring_copy(step, way, sent_chunk(step, way, core)).wait_send()
            share_copy(step, way, core).wait_send()
            share_copy(step, way, 1 - core).wait_recv()
    width = rotation_ref.shape[1]

    def turn(pair, carry):
        wide = jnp.concatenate([columns[2 * pair], columns[2 * pair + 1]], axis=1)
        where = pl.ds(pl.multiple_of(pair * 2 * width, 128), 2 * width)
        rotated_ref[:, where] = jnp.dot(
            owned_ref[...], wide, preferred_element_type=jnp.float32
        ).astype(jnp.bfloat16)
        return carry

    lax.fori_loop(0, owners // 2, turn, 0)


def per_device_pair(start_bands, hamiltonian, neighbours, basis_count, owner_rows, rotation):
    bands_dev, rows_dev = start_bands.shape
    owners = lax.axis_size("band")
    cap = 3 * rows_dev // owners
    bands_all, width = rotation.shape
    hops = owners // 2 - 1
    vmem = pl.BlockSpec(memory_space=pltpu.VMEM)
    smem = pl.BlockSpec(memory_space=pltpu.SMEM)
    dma = pltpu.SemaphoreType.DMA
    bf16 = jnp.bfloat16
    return pl.pallas_call(
        functools.partial(filter_kernel, owners),
        out_shape=(
            jax.ShapeDtypeStruct((bands_dev, rows_dev), bf16),
            jax.ShapeDtypeStruct((cap, owners * width), bf16),
        ),
        in_specs=[vmem, vmem, smem, smem, smem, vmem],
        out_specs=(vmem, vmem),
        scratch_shapes=[
            pltpu.VMEM((cap, bands_all), bf16),
            pltpu.VMEM((owners, bands_all, width), bf16),
            pltpu.VMEM((2, 2 * rows_dev, rows_dev), bf16),
            pltpu.VMEM((2, bands_dev // 2, 2 * rows_dev), bf16),
            pltpu.VMEM((bands_dev, rows_dev), bf16),
            pltpu.VMEM((bands_dev // 2, rows_dev), bf16),
            pltpu.VMEM((owners, cap, bands_dev), bf16),
            pltpu.VMEM((owners, cap, bands_dev), bf16),
            dma,
            dma,
            dma((4,)),
            dma((4,)),
            dma((4,)),
            dma((4,)),
            dma,
            dma,
            dma((owners,)),
            dma((owners,)),
            dma((2, hops)),
            dma((2, hops)),
            dma((2, hops)),
            dma((2, hops)),
            dma,
            dma,
        ],
        compiler_params=pltpu.CompilerParams(
            collective_id=0, has_side_effects=True, vmem_limit_bytes=40 * 1024 * 1024
        ),
        cost_estimate=pl.CostEstimate(
            flops=16 * bands_dev * 2 * rows_dev * rows_dev,
            bytes_accessed=200_000_000,
            transcendentals=0,
        ),
    )(start_bands, hamiltonian, neighbours, basis_count, owner_rows, rotation)


def solution(mesh):
    pair = mesh.shape["elem"] == 2 and mesh.shape["band"] % 4 == 0
    placed = (
        P("band", "elem"),
        P("elem", None, None, None),
        P("elem", None),
        P("elem"),
        P(),
        P(None, "band"),
    )
    return jax.shard_map(
        per_device_pair if pair else per_device,
        mesh=mesh,
        in_specs=placed,
        out_specs=(P("band", "elem"), P(("elem", "band"), None)),
        check_vma=False,
    )
```

```python
import functools

import jax
import jax.numpy as jnp
from jax import lax
from jax.experimental import pallas as pl
from jax.experimental.pallas import tpu as pltpu
from jax.sharding import PartitionSpec as P

DEGREE = 8


def padded_2(block, sides, width):
    for axis, dim in sides:
        count = lax.axis_size(axis)
        forward = [(i, i + 1) for i in range(count - 1)]
        forward.append((count - 1, 0))
        backward = [(target, source) for source, target in forward]
        low = lax.ppermute(
            lax.slice_in_dim(block, block.shape[dim] - width, None, axis=dim), axis, forward
        )
        high = lax.ppermute(lax.slice_in_dim(block, 0, width, axis=dim), axis, backward)
        block = jnp.concatenate([low, block, high], axis=dim)
    return block


def per_device(start_bands, hamiltonian, neighbours, basis_count, owner_rows, rotation):
    bands_dev, rows_dev = start_bands.shape
    elem_count = hamiltonian.shape[0]
    basis_max = hamiltonian.shape[2]
    planes_dev = elem_count // 4
    basis_ids = lax.broadcasted_iota(jnp.int32, (elem_count, basis_max), 1)
    row_mask = (basis_ids < basis_count[:, None]).astype(jnp.float32).reshape(rows_dev)
    partner_pick = (neighbours[:, :, None] == jnp.arange(4, dtype=jnp.int32)[None, None, :]).astype(
        jnp.bfloat16
    )
    partner_pick = partner_pick.reshape(planes_dev, 4, 6, 4)
    weights = hamiltonian.reshape(elem_count, 7 * basis_max, basis_max)

    def apply_ham(state):
        plane_slab = state.reshape(bands_dev, planes_dev, 4 * basis_max)
        extended = padded_2(plane_slab, (("elem", 1),), 1)
        extended = extended.reshape(bands_dev, planes_dev + 2, 4, basis_max)
        plane_below = extended[:, :planes_dev]
        plane_mid = extended[:, 1 : planes_dev + 1]
        plane_above = extended[:, 2:]
        inplane = jnp.einsum(
            "pism,bpmk->bpisk",
            partner_pick[:, :, :4],
            plane_mid,
            preferred_element_type=jnp.float32,
        ).astype(jnp.bfloat16)
        lower = jnp.einsum(
            "pim,bpmk->bpik", partner_pick[:, :, 4], plane_below, preferred_element_type=jnp.float32
        ).astype(jnp.bfloat16)
        upper = jnp.einsum(
            "pim,bpmk->bpik", partner_pick[:, :, 5], plane_above, preferred_element_type=jnp.float32
        ).astype(jnp.bfloat16)
        sources = jnp.concatenate(
            [plane_mid[:, :, :, None], inplane, lower[:, :, :, None], upper[:, :, :, None]], axis=3
        )
        sources = sources.reshape(bands_dev, elem_count, 7 * basis_max)
        product = jnp.einsum("bej,ejl->bel", sources, weights, preferred_element_type=jnp.float32)
        return product.reshape(bands_dev, rows_dev) * row_mask

    earlier = (start_bands.astype(jnp.float32) * row_mask).astype(jnp.bfloat16)
    current = (0.5 * apply_ham(earlier)).astype(jnp.bfloat16)
    for repeat in range(DEGREE - 1):
        following = (apply_ham(current) - earlier.astype(jnp.float32)).astype(jnp.bfloat16)
        earlier = current
        current = following
    owners = lax.axis_size("band")
    slot_cap = 3 * rows_dev // owners
    before = jnp.arange(owners)[None, :] < jnp.arange(owners)[:, None]
    row_starts = jnp.sum(jnp.where(before, owner_rows[None, :], 0), axis=1)
    slot_keep = jnp.arange(slot_cap, dtype=jnp.int32)[None, :] < owner_rows[:, None]
    padded = jnp.concatenate([current, jnp.zeros((bands_dev, slot_cap), jnp.bfloat16)], axis=1)
    pieces = jax.vmap(lambda offset: lax.dynamic_slice_in_dim(padded, offset, slot_cap, 1))(
        row_starts
    )
    owned_rows = lax.all_to_all(
        jnp.where(slot_keep[:, None, :], pieces, jnp.zeros((), jnp.bfloat16)),
        "band",
        split_axis=0,
        concat_axis=1,
        tiled=True,
    ).reshape(-1, slot_cap)
    rotated = lax.dot_general(
        owned_rows,
        lax.all_gather(rotation, "band", axis=1, tiled=True),
        (((0,), (0,)), ((), ())),
        preferred_element_type=jnp.float32,
    ).astype(jnp.bfloat16)
    return (current, rotated)


def filter_kernel(
    owners,
    start_hbm,
    ham_hbm,
    nb_ref,
    count_ref,
    owner_ref,
    rotation_hbm,
    filtered_ref,
    rotated_ref,
    owned_ref,
    columns,
    amat,
    bands,
    masked,
    swapped,
    pieces,
    arrived,
    band_send,
    band_recv,
    strip_send,
    strip_recv,
    core_send,
    core_recv,
    back_send,
    back_recv,
    piece_send,
    piece_recv,
    ring_send,
    ring_recv,
    share_send,
    share_recv,
    mine_send,
    mine_recv,
    start_ref,
    ham_ref,
    load_sem,
    side_send,
    side_recv,
    second_send,
    second_recv,
):
    e = lax.axis_index("elem")
    b = lax.axis_index("band")
    o = 1 - e
    core = lax.rem(b, 2)
    sib = b + 1 - 2 * core
    load_rotation = pltpu.make_async_copy(rotation_hbm, columns.at[b], load_sem.at[0])
    load_start = pltpu.make_async_copy(start_hbm, start_ref, load_sem.at[1])
    load_ham = pltpu.make_async_copy(ham_hbm, ham_ref, load_sem.at[2])
    load_rotation.start()
    load_start.start()
    load_ham.start()
    count, rows = start_ref.shape
    half = count // 2
    nb = ham_ref.shape[2]
    cap = owned_ref.shape[0]

    barrier = pltpu.get_barrier_semaphore()
    pl.semaphore_signal(barrier, inc=1, device_id={"elem": o}, device_id_type=pl.DeviceIdType.MESH)

    def greet(d, carry):
        j = lax.rem(b + d, owners)
        pl.semaphore_signal(
            barrier, inc=1, device_id={"band": j}, device_id_type=pl.DeviceIdType.MESH
        )
        return carry

    lax.fori_loop(1, owners, greet, 0)
    pl.semaphore_wait(barrier, owners)

    chips = owners // 2
    tall = chips // 2
    chip = b // 2
    layer = chip // 2
    place = jnp.where(lax.rem(chip, 2) == 0, layer, chips - 1 - layer)
    depth = rotation_hbm.shape[0] // 2

    def member(position, which):
        position = lax.rem(position + 2 * chips, chips)
        near = 4 * position
        far = 4 * (chips - 1 - position) + 2
        return jnp.where(position < tall, near, far) + which

    def part(chunk, way):
        return columns.at[chunk, pl.ds(way * depth, depth)]

    def ring_copy(step, way, chunk):
        return pltpu.make_async_remote_copy(
            src_ref=part(chunk, way),
            dst_ref=part(chunk, way),
            send_sem=ring_send.at[way, step],
            recv_sem=ring_recv.at[way, step],
            device_id={"band": member(place + 1 - 2 * way, core)},
            device_id_type=pl.DeviceIdType.MESH,
        )

    def sent_chunk(step, way, which):
        return member(place - step + 2 * step * way, which)

    def share_copy(step, way, which):
        chunk = sent_chunk(step + 1, way, which)
        return pltpu.make_async_remote_copy(
            src_ref=part(chunk, way),
            dst_ref=part(chunk, way),
            send_sem=share_send.at[way, step],
            recv_sem=share_recv.at[way, step],
            device_id={"band": sib},
            device_id_type=pl.DeviceIdType.MESH,
        )

    def mine_copy(chunk):
        return pltpu.make_async_remote_copy(
            src_ref=columns.at[chunk],
            dst_ref=columns.at[chunk],
            send_sem=mine_send,
            recv_sem=mine_recv,
            device_id={"band": sib},
            device_id_type=pl.DeviceIdType.MESH,
        )

    def ring(step):
        for way in range(2):
            if step > 0:
                ring_copy(step - 1, way, sent_chunk(step, way, core)).wait_recv()
            if step < chips - 1:
                ring_copy(step, way, sent_chunk(step, way, core)).start()
            if step > 0:
                share_copy(step - 1, way, core).start()

    passed = [0]

    def ring_next():
        if passed[0] < chips - 1:
            passed[0] += 1
            ring(passed[0])

    load_rotation.wait()
    ring(0)
    mine_copy(b).start()
    load_start.wait()

    lane = lax.broadcasted_iota(jnp.int32, (1, rows), 1)
    keep = jnp.zeros((1, rows), jnp.float32)
    for i in range(4):
        inside = (lane >= nb * i) & (lane < nb * i + count_ref[i])
        keep = jnp.where(inside, 1.0, keep)
    masked[...] = (start_ref[...].astype(jnp.float32) * keep).astype(jnp.bfloat16)
    own_cols = pl.ds(pl.multiple_of(rows * e, 128), rows)
    other_cols = pl.ds(pl.multiple_of(rows * o, 128), rows)
    own_half = pl.ds(pl.multiple_of(half * e, 16), half)
    other_half = pl.ds(pl.multiple_of(half * o, 16), half)
    band_copy = pltpu.make_async_remote_copy(
        src_ref=masked.at[other_half],
        dst_ref=bands.at[0, :, own_cols],
        send_sem=band_send,
        recv_sem=band_recv,
        device_id={"elem": o},
        device_id_type=pl.DeviceIdType.MESH,
    )
    band_copy.start()
    bands[0, :, own_cols] = masked[own_half, :]

    thin = nb // 2
    beside = lax.rem(chip, 2)
    quarter = 2 * beside + core
    beside_quarter = 2 * (1 - beside) + core
    across = b + 2 - 4 * beside

    def strip_rows(t):
        return pl.ds(pl.multiple_of(t * nb, 16), nb)

    def thin_rows(step, which):
        return pl.ds(pl.multiple_of(2 * nb * which + step * thin, 16), thin)

    def build(t):
        parts = []
        for i in range(4):
            total = jnp.where(t == 4 * e + i, 1.0, 0.0) * ham_ref[i, 0].astype(jnp.float32)
            for j in range(1, 7):
                plane = e if j < 5 else o
                pick = jnp.where(nb_ref[i, j - 1] + 4 * plane == t, 1.0, 0.0)
                total = total + pick * ham_ref[i, j].astype(jnp.float32)
            parts.append(total)
        strip = jnp.concatenate(parts, axis=1) * keep
        amat[e, strip_rows(t), :] = strip.astype(jnp.bfloat16)

    def move(plane, step, which, send, recv, device):
        where = thin_rows(step, which)
        return pltpu.make_async_remote_copy(
            src_ref=amat.at[plane, where],
            dst_ref=amat.at[plane, where],
            send_sem=send.at[step],
            recv_sem=recv.at[step],
            device_id=device,
            device_id_type=pl.DeviceIdType.MESH,
        )

    def to_partner(step):
        return move(e, step, quarter, strip_send, strip_recv, {"elem": o})

    def from_partner(step):
        return move(o, step, quarter, strip_send, strip_recv, {"elem": o})

    def to_side(step, which):
        return move(o, step, which, side_send, side_recv, {"band": across})

    def to_sibling(step, which):
        return move(o, step, which, core_send, core_recv, {"band": sib})

    def second_to_sibling(step, which):
        return move(o, step, which, second_send, second_recv, {"band": sib})

    def first_build(step, carry):
        build(2 * quarter + step)
        for k in range(2):
            to_partner(2 * step + k).start()
        return carry

    def other_build(step, carry):
        build(lax.rem(2 * quarter + step, 8))
        return carry

    def forward(step):
        from_partner(step).wait_recv()
        to_side(step, quarter).start()
        to_sibling(step, quarter).start()

    def second_forward(step):
        to_side(step, beside_quarter).wait_recv()
        second_to_sibling(step, beside_quarter).start()

    def collect(step, carry):
        to_sibling(step, 2 * beside + 1 - core).wait_recv()
        second_to_sibling(step, 2 * (1 - beside) + 1 - core).wait_recv()
        to_partner(step).wait_send()
        to_side(step, quarter).wait_send()
        to_sibling(step, quarter).wait_send()
        second_to_sibling(step, beside_quarter).wait_send()
        return carry

    load_ham.wait()
    lax.fori_loop(0, 2, first_build, 0)
    lax.fori_loop(2, 8, other_build, 0)
    forward(0)
    forward(1)
    ring_next()
    forward(2)
    second_forward(0)
    forward(3)
    second_forward(1)
    ring_next()
    second_forward(2)
    second_forward(3)
    lax.fori_loop(0, 4, collect, 0)
    band_copy.wait_send()
    pltpu.make_async_remote_copy(
        src_ref=masked.at[other_half],
        dst_ref=bands.at[0, :, other_cols],
        send_sem=band_send,
        recv_sem=band_recv,
        device_id={"elem": o},
        device_id_type=pl.DeviceIdType.MESH,
    ).wait_recv()

    wide = 256 if rows % 256 == 0 else rows

    def advance(now, later, first):
        for p in range(2):
            for c in range(rows // wide):
                product = jnp.dot(
                    bands[now],
                    amat[p, :, c * wide : (c + 1) * wide],
                    preferred_element_type=jnp.float32,
                )
                cols = slice(p * rows + c * wide, p * rows + (c + 1) * wide)
                if first:
                    product = 0.5 * product
                else:
                    product = product - bands[later, :, cols].astype(jnp.float32)
                bands[later, :, cols] = product.astype(jnp.bfloat16)

    advance(0, 1, True)

    def two_steps(k, carry):
        advance(1, 0, False)
        advance(0, 1, False)
        return carry

    split = (DEGREE - 2) // 4
    lax.fori_loop(0, split, two_steps, 0)
    ring_next()
    lax.fori_loop(split, (DEGREE - 2) // 2, two_steps, 0)
    ring_next()
    advance(1, 0, False)

    back = pltpu.make_async_remote_copy(
        src_ref=bands.at[0, :, other_cols],
        dst_ref=swapped,
        send_sem=back_send,
        recv_sem=back_recv,
        device_id={"elem": o},
        device_id_type=pl.DeviceIdType.MESH,
    )
    back.start()
    ring_next()
    masked[own_half, :] = bands[0, :, own_cols]
    back.wait()
    masked[other_half, :] = swapped[...]
    filtered_ref[...] = masked[...]

    lanes = lax.broadcasted_iota(jnp.int32, (cap, rows), 1)
    slots = lax.broadcasted_iota(jnp.int32, (cap, rows), 0)

    def piece(j):
        begin = jnp.int32(0)
        for i in range(owners):
            begin = begin + jnp.where(i < j, owner_ref[i], 0)
        chosen = (lanes == slots + begin) & (slots < owner_ref[j])
        pick = jnp.where(chosen, 1.0, 0.0).astype(jnp.bfloat16)
        return lax.dot_general(
            pick, masked[...], (((1,), (1,)), ((), ())), preferred_element_type=jnp.float32
        ).astype(jnp.bfloat16)

    def piece_copy(j, origin):
        return pltpu.make_async_remote_copy(
            src_ref=pieces.at[j],
            dst_ref=arrived.at[origin],
            send_sem=piece_send.at[j],
            recv_sem=piece_recv.at[origin],
            device_id={"band": j},
            device_id_type=pl.DeviceIdType.MESH,
        )

    def send(d, carry):
        j = lax.rem(b + d, owners)
        pieces[j] = piece(j)
        piece_copy(j, b).start()
        return carry

    lax.fori_loop(1, owners // 2, send, 0)
    ring_next()
    lax.fori_loop(owners // 2, owners, send, 0)
    arrived[b] = piece(b)

    def receive(d, carry):
        j = lax.rem(b + d, owners)
        piece_copy(j, j).wait_recv()
        piece_copy(j, b).wait_send()
        return carry

    while passed[0] < chips - 1:
        ring_next()
    lax.fori_loop(1, owners, receive, 0)
    for i in range(owners):
        owned_ref[:, i * count : (i + 1) * count] = arrived[i]
    mine_copy(b).wait_send()
    mine_copy(sib).wait_recv()
    for step in range(chips - 1):
        for way in range(2):
            ring_copy(step, way, sent_chunk(step, way, core)).wait_send()
            share_copy(step, way, core).wait_send()
            share_copy(step, way, 1 - core).wait_recv()
    width = rotation_hbm.shape[1]

    def turn(pair, carry):
        wide = jnp.concatenate([columns[2 * pair], columns[2 * pair + 1]], axis=1)
        where = pl.ds(pl.multiple_of(pair * 2 * width, 128), 2 * width)
        rotated_ref[:, where] = jnp.dot(
            owned_ref[...], wide, preferred_element_type=jnp.float32
        ).astype(jnp.bfloat16)
        return carry

    lax.fori_loop(0, owners // 2, turn, 0)


def per_device_pair(start_bands, hamiltonian, neighbours, basis_count, owner_rows, rotation):
    bands_dev, rows_dev = start_bands.shape
    owners = lax.axis_size("band")
    cap = 3 * rows_dev // owners
    bands_all, width = rotation.shape
    hops = owners // 2 - 1
    vmem = pl.BlockSpec(memory_space=pltpu.VMEM)
    hbm = pl.BlockSpec(memory_space=pltpu.HBM)
    smem = pl.BlockSpec(memory_space=pltpu.SMEM)
    dma = pltpu.SemaphoreType.DMA
    bf16 = jnp.bfloat16
    return pl.pallas_call(
        functools.partial(filter_kernel, owners),
        out_shape=(
            jax.ShapeDtypeStruct((bands_dev, rows_dev), bf16),
            jax.ShapeDtypeStruct((cap, owners * width), bf16),
        ),
        in_specs=[hbm, hbm, smem, smem, smem, hbm],
        out_specs=(vmem, vmem),
        scratch_shapes=[
            pltpu.VMEM((cap, bands_all), bf16),
            pltpu.VMEM((owners, bands_all, width), bf16),
            pltpu.VMEM((2, 2 * rows_dev, rows_dev), bf16),
            pltpu.VMEM((2, bands_dev // 2, 2 * rows_dev), bf16),
            pltpu.VMEM((bands_dev, rows_dev), bf16),
            pltpu.VMEM((bands_dev // 2, rows_dev), bf16),
            pltpu.VMEM((owners, cap, bands_dev), bf16),
            pltpu.VMEM((owners, cap, bands_dev), bf16),
            dma,
            dma,
            dma((4,)),
            dma((4,)),
            dma((4,)),
            dma((4,)),
            dma,
            dma,
            dma((owners,)),
            dma((owners,)),
            dma((2, hops)),
            dma((2, hops)),
            dma((2, hops)),
            dma((2, hops)),
            dma,
            dma,
            pltpu.VMEM(start_bands.shape, bf16),
            pltpu.VMEM(hamiltonian.shape, bf16),
            dma((3,)),
            dma((4,)),
            dma((4,)),
            dma((4,)),
            dma((4,)),
        ],
        compiler_params=pltpu.CompilerParams(
            collective_id=0, has_side_effects=True, vmem_limit_bytes=40 * 1024 * 1024
        ),
        cost_estimate=pl.CostEstimate(
            flops=16 * bands_dev * 2 * rows_dev * rows_dev,
            bytes_accessed=200_000_000,
            transcendentals=0,
        ),
    )(start_bands, hamiltonian, neighbours, basis_count, owner_rows, rotation)


def solution(mesh):
    pair = mesh.shape["elem"] == 2 and mesh.shape["band"] % 4 == 0
    placed = (
        P("band", "elem"),
        P("elem", None, None, None),
        P("elem", None),
        P("elem"),
        P(),
        P(None, "band"),
    )
    return jax.shard_map(
        per_device_pair if pair else per_device,
        mesh=mesh,
        in_specs=placed,
        out_specs=(P("band", "elem"), P(("elem", "band"), None)),
        check_vma=False,
    )
```

```python
import functools

import jax
import jax.numpy as jnp
from jax import lax
from jax.experimental import pallas as pl
from jax.experimental.pallas import tpu as pltpu
from jax.sharding import PartitionSpec as P

DEGREE = 8


def padded_2(block, sides, width):
    for axis, dim in sides:
        count = lax.axis_size(axis)
        forward = [(i, i + 1) for i in range(count - 1)]
        forward.append((count - 1, 0))
        backward = [(target, source) for source, target in forward]
        low = lax.ppermute(
            lax.slice_in_dim(block, block.shape[dim] - width, None, axis=dim), axis, forward
        )
        high = lax.ppermute(lax.slice_in_dim(block, 0, width, axis=dim), axis, backward)
        block = jnp.concatenate([low, block, high], axis=dim)
    return block


def per_device(start_bands, hamiltonian, neighbours, basis_count, owner_rows, rotation):
    bands_dev, rows_dev = start_bands.shape
    elem_count = hamiltonian.shape[0]
    basis_max = hamiltonian.shape[2]
    planes_dev = elem_count // 4
    basis_ids = lax.broadcasted_iota(jnp.int32, (elem_count, basis_max), 1)
    row_mask = (basis_ids < basis_count[:, None]).astype(jnp.float32).reshape(rows_dev)
    partner_pick = (neighbours[:, :, None] == jnp.arange(4, dtype=jnp.int32)[None, None, :]).astype(
        jnp.bfloat16
    )
    partner_pick = partner_pick.reshape(planes_dev, 4, 6, 4)
    weights = hamiltonian.reshape(elem_count, 7 * basis_max, basis_max)

    def apply_ham(state):
        plane_slab = state.reshape(bands_dev, planes_dev, 4 * basis_max)
        extended = padded_2(plane_slab, (("elem", 1),), 1)
        extended = extended.reshape(bands_dev, planes_dev + 2, 4, basis_max)
        plane_below = extended[:, :planes_dev]
        plane_mid = extended[:, 1 : planes_dev + 1]
        plane_above = extended[:, 2:]
        inplane = jnp.einsum(
            "pism,bpmk->bpisk",
            partner_pick[:, :, :4],
            plane_mid,
            preferred_element_type=jnp.float32,
        ).astype(jnp.bfloat16)
        lower = jnp.einsum(
            "pim,bpmk->bpik", partner_pick[:, :, 4], plane_below, preferred_element_type=jnp.float32
        ).astype(jnp.bfloat16)
        upper = jnp.einsum(
            "pim,bpmk->bpik", partner_pick[:, :, 5], plane_above, preferred_element_type=jnp.float32
        ).astype(jnp.bfloat16)
        sources = jnp.concatenate(
            [plane_mid[:, :, :, None], inplane, lower[:, :, :, None], upper[:, :, :, None]], axis=3
        )
        sources = sources.reshape(bands_dev, elem_count, 7 * basis_max)
        product = jnp.einsum("bej,ejl->bel", sources, weights, preferred_element_type=jnp.float32)
        return product.reshape(bands_dev, rows_dev) * row_mask

    earlier = (start_bands.astype(jnp.float32) * row_mask).astype(jnp.bfloat16)
    current = (0.5 * apply_ham(earlier)).astype(jnp.bfloat16)
    for repeat in range(DEGREE - 1):
        following = (apply_ham(current) - earlier.astype(jnp.float32)).astype(jnp.bfloat16)
        earlier = current
        current = following
    owners = lax.axis_size("band")
    slot_cap = 3 * rows_dev // owners
    before = jnp.arange(owners)[None, :] < jnp.arange(owners)[:, None]
    row_starts = jnp.sum(jnp.where(before, owner_rows[None, :], 0), axis=1)
    slot_keep = jnp.arange(slot_cap, dtype=jnp.int32)[None, :] < owner_rows[:, None]
    padded = jnp.concatenate([current, jnp.zeros((bands_dev, slot_cap), jnp.bfloat16)], axis=1)
    pieces = jax.vmap(lambda offset: lax.dynamic_slice_in_dim(padded, offset, slot_cap, 1))(
        row_starts
    )
    owned_rows = lax.all_to_all(
        jnp.where(slot_keep[:, None, :], pieces, jnp.zeros((), jnp.bfloat16)),
        "band",
        split_axis=0,
        concat_axis=1,
        tiled=True,
    ).reshape(-1, slot_cap)
    rotated = lax.dot_general(
        owned_rows,
        lax.all_gather(rotation, "band", axis=1, tiled=True),
        (((0,), (0,)), ((), ())),
        preferred_element_type=jnp.float32,
    ).astype(jnp.bfloat16)
    return (current, rotated)


def filter_kernel(
    owners,
    start_ref,
    ham_ref,
    nb_ref,
    count_ref,
    owner_ref,
    rotation_ref,
    filtered_ref,
    rotated_ref,
    owned_ref,
    columns,
    amat,
    bands,
    masked,
    swapped,
    pieces,
    arrived,
    band_send,
    band_recv,
    strip_send,
    strip_recv,
    core_send,
    core_recv,
    back_send,
    back_recv,
    piece_send,
    piece_recv,
    ring_send,
    ring_recv,
    share_send,
    share_recv,
    mine_send,
    mine_recv,
):
    e = lax.axis_index("elem")
    b = lax.axis_index("band")
    o = 1 - e
    core = lax.rem(b, 2)
    sib = b + 1 - 2 * core
    count, rows = start_ref.shape
    half = count // 2
    nb = ham_ref.shape[2]
    cap = owned_ref.shape[0]

    barrier = pltpu.get_barrier_semaphore()
    pl.semaphore_signal(barrier, inc=1, device_id={"elem": o}, device_id_type=pl.DeviceIdType.MESH)

    def greet(d, carry):
        j = lax.rem(b + d, owners)
        pl.semaphore_signal(
            barrier, inc=1, device_id={"band": j}, device_id_type=pl.DeviceIdType.MESH
        )
        return carry

    lax.fori_loop(1, owners, greet, 0)
    pl.semaphore_wait(barrier, owners)

    chips = owners // 2
    tall = chips // 2
    chip = b // 2
    layer = chip // 2
    place = jnp.where(lax.rem(chip, 2) == 0, layer, chips - 1 - layer)
    depth = rotation_ref.shape[0] // 2

    def member(position, which):
        position = lax.rem(position + 2 * chips, chips)
        near = 4 * position
        far = 4 * (chips - 1 - position) + 2
        return jnp.where(position < tall, near, far) + which

    def part(chunk, way):
        return columns.at[chunk, pl.ds(way * depth, depth)]

    def ring_copy(step, way, chunk):
        return pltpu.make_async_remote_copy(
            src_ref=part(chunk, way),
            dst_ref=part(chunk, way),
            send_sem=ring_send.at[way, step],
            recv_sem=ring_recv.at[way, step],
            device_id={"band": member(place + 1 - 2 * way, core)},
            device_id_type=pl.DeviceIdType.MESH,
        )

    def sent_chunk(step, way, which):
        return member(place - step + 2 * step * way, which)

    def share_copy(step, way, which):
        chunk = sent_chunk(step + 1, way, which)
        return pltpu.make_async_remote_copy(
            src_ref=part(chunk, way),
            dst_ref=part(chunk, way),
            send_sem=share_send.at[way, step],
            recv_sem=share_recv.at[way, step],
            device_id={"band": sib},
            device_id_type=pl.DeviceIdType.MESH,
        )

    def mine_copy(chunk):
        return pltpu.make_async_remote_copy(
            src_ref=columns.at[chunk],
            dst_ref=columns.at[chunk],
            send_sem=mine_send,
            recv_sem=mine_recv,
            device_id={"band": sib},
            device_id_type=pl.DeviceIdType.MESH,
        )

    def ring(step):
        for way in range(2):
            if step > 0:
                ring_copy(step - 1, way, sent_chunk(step, way, core)).wait_recv()
            if step < chips - 1:
                ring_copy(step, way, sent_chunk(step, way, core)).start()
            if step > 0:
                share_copy(step - 1, way, core).start()

    columns[b] = rotation_ref[...]
    passed = [0]

    def ring_next():
        if passed[0] < chips - 1:
            passed[0] += 1
            ring(passed[0])

    ring(0)
    mine_copy(b).start()

    lane = lax.broadcasted_iota(jnp.int32, (1, rows), 1)
    keep = jnp.zeros((1, rows), jnp.float32)
    for i in range(4):
        inside = (lane >= nb * i) & (lane < nb * i + count_ref[i])
        keep = jnp.where(inside, 1.0, keep)
    masked[...] = (start_ref[...].astype(jnp.float32) * keep).astype(jnp.bfloat16)
    own_cols = pl.ds(pl.multiple_of(rows * e, 128), rows)
    other_cols = pl.ds(pl.multiple_of(rows * o, 128), rows)
    own_half = pl.ds(pl.multiple_of(half * e, 16), half)
    other_half = pl.ds(pl.multiple_of(half * o, 16), half)
    band_copy = pltpu.make_async_remote_copy(
        src_ref=masked.at[other_half],
        dst_ref=bands.at[0, :, own_cols],
        send_sem=band_send,
        recv_sem=band_recv,
        device_id={"elem": o},
        device_id_type=pl.DeviceIdType.MESH,
    )
    band_copy.start()
    bands[0, :, own_cols] = masked[own_half, :]

    def strip_rows(step, side):
        t = 4 * side + step
        return pl.ds(pl.multiple_of(t * nb, 16), nb)

    def build(step, side):
        t = 4 * side + step
        parts = []
        for i in range(4):
            total = jnp.where(t == 4 * e + i, 1.0, 0.0) * ham_ref[i, 0].astype(jnp.float32)
            for j in range(1, 7):
                plane = e if j < 5 else o
                pick = jnp.where(nb_ref[i, j - 1] + 4 * plane == t, 1.0, 0.0)
                total = total + pick * ham_ref[i, j].astype(jnp.float32)
            parts.append(total)
        strip = jnp.concatenate(parts, axis=1) * keep
        amat[e, strip_rows(step, side), :] = strip.astype(jnp.bfloat16)

    def to_partner(step):
        where = strip_rows(step, core)
        return pltpu.make_async_remote_copy(
            src_ref=amat.at[e, where],
            dst_ref=amat.at[e, where],
            send_sem=strip_send.at[step],
            recv_sem=strip_recv.at[step],
            device_id={"elem": o},
            device_id_type=pl.DeviceIdType.MESH,
        )

    def from_partner(step):
        where = strip_rows(step, core)
        return pltpu.make_async_remote_copy(
            src_ref=amat.at[o, where],
            dst_ref=amat.at[o, where],
            send_sem=strip_send.at[step],
            recv_sem=strip_recv.at[step],
            device_id={"elem": o},
            device_id_type=pl.DeviceIdType.MESH,
        )

    def to_sibling(step, side):
        where = strip_rows(step, side)
        return pltpu.make_async_remote_copy(
            src_ref=amat.at[o, where],
            dst_ref=amat.at[o, where],
            send_sem=core_send.at[step],
            recv_sem=core_recv.at[step],
            device_id={"band": sib},
            device_id_type=pl.DeviceIdType.MESH,
        )

    def first_half(step, carry):
        build(step, core)
        to_partner(step).start()
        return carry

    def second_half(step, carry):
        build(step, 1 - core)
        return carry

    def forward(step, carry):
        from_partner(step).wait_recv()
        to_sibling(step, core).start()
        return carry

    def collect(step, carry):
        to_sibling(step, 1 - core).wait_recv()
        to_sibling(step, core).wait_send()
        to_partner(step).wait_send()
        return carry

    lax.fori_loop(0, 4, first_half, 0)
    lax.fori_loop(0, 4, second_half, 0)
    for step in range(4):
        forward(step, 0)
        ring_next()
    lax.fori_loop(0, 4, collect, 0)
    band_copy.wait_send()
    pltpu.make_async_remote_copy(
        src_ref=masked.at[other_half],
        dst_ref=bands.at[0, :, other_cols],
        send_sem=band_send,
        recv_sem=band_recv,
        device_id={"elem": o},
        device_id_type=pl.DeviceIdType.MESH,
    ).wait_recv()

    wide = 256 if rows % 256 == 0 else rows

    def advance(now, later, first):
        for p in range(2):
            for c in range(rows // wide):
                product = jnp.dot(
                    bands[now],
                    amat[p, :, c * wide : (c + 1) * wide],
                    preferred_element_type=jnp.float32,
                )
                cols = slice(p * rows + c * wide, p * rows + (c + 1) * wide)
                if first:
                    product = 0.5 * product
                else:
                    product = product - bands[later, :, cols].astype(jnp.float32)
                bands[later, :, cols] = product.astype(jnp.bfloat16)

    advance(0, 1, True)

    def two_steps(k, carry):
        advance(1, 0, False)
        advance(0, 1, False)
        return carry

    split = (DEGREE - 2) // 4
    lax.fori_loop(0, split, two_steps, 0)
    ring_next()
    lax.fori_loop(split, (DEGREE - 2) // 2, two_steps, 0)
    advance(1, 0, False)

    back = pltpu.make_async_remote_copy(
        src_ref=bands.at[0, :, other_cols],
        dst_ref=swapped,
        send_sem=back_send,
        recv_sem=back_recv,
        device_id={"elem": o},
        device_id_type=pl.DeviceIdType.MESH,
    )
    back.start()
    ring_next()
    masked[own_half, :] = bands[0, :, own_cols]
    back.wait()
    masked[other_half, :] = swapped[...]
    filtered_ref[...] = masked[...]

    lanes = lax.broadcasted_iota(jnp.int32, (cap, rows), 1)
    slots = lax.broadcasted_iota(jnp.int32, (cap, rows), 0)

    def piece(j):
        begin = jnp.int32(0)
        for i in range(owners):
            begin = begin + jnp.where(i < j, owner_ref[i], 0)
        chosen = (lanes == slots + begin) & (slots < owner_ref[j])
        pick = jnp.where(chosen, 1.0, 0.0).astype(jnp.bfloat16)
        return lax.dot_general(
            pick, masked[...], (((1,), (1,)), ((), ())), preferred_element_type=jnp.float32
        ).astype(jnp.bfloat16)

    def piece_copy(j, origin):
        return pltpu.make_async_remote_copy(
            src_ref=pieces.at[j],
            dst_ref=arrived.at[origin],
            send_sem=piece_send.at[j],
            recv_sem=piece_recv.at[origin],
            device_id={"band": j},
            device_id_type=pl.DeviceIdType.MESH,
        )

    def send(d, carry):
        j = lax.rem(b + d, owners)
        pieces[j] = piece(j)
        piece_copy(j, b).start()
        return carry

    lax.fori_loop(1, owners, send, 0)
    arrived[b] = piece(b)

    def receive(d, carry):
        j = lax.rem(b + d, owners)
        piece_copy(j, j).wait_recv()
        piece_copy(j, b).wait_send()
        return carry

    while passed[0] < chips - 1:
        ring_next()
    lax.fori_loop(1, owners, receive, 0)
    for i in range(owners):
        owned_ref[:, i * count : (i + 1) * count] = arrived[i]
    mine_copy(b).wait_send()
    mine_copy(sib).wait_recv()
    for step in range(chips - 1):
        for way in range(2):
            ring_copy(step, way, sent_chunk(step, way, core)).wait_send()
            share_copy(step, way, core).wait_send()
            share_copy(step, way, 1 - core).wait_recv()
    width = rotation_ref.shape[1]

    def turn(pair, carry):
        wide = jnp.concatenate([columns[2 * pair], columns[2 * pair + 1]], axis=1)
        where = pl.ds(pl.multiple_of(pair * 2 * width, 128), 2 * width)
        rotated_ref[:, where] = jnp.dot(
            owned_ref[...], wide, preferred_element_type=jnp.float32
        ).astype(jnp.bfloat16)
        return carry

    lax.fori_loop(0, owners // 2, turn, 0)


def per_device_pair(start_bands, hamiltonian, neighbours, basis_count, owner_rows, rotation):
    bands_dev, rows_dev = start_bands.shape
    owners = lax.axis_size("band")
    cap = 3 * rows_dev // owners
    bands_all, width = rotation.shape
    hops = owners // 2 - 1
    vmem = pl.BlockSpec(memory_space=pltpu.VMEM)
    smem = pl.BlockSpec(memory_space=pltpu.SMEM)
    dma = pltpu.SemaphoreType.DMA
    bf16 = jnp.bfloat16
    return pl.pallas_call(
        functools.partial(filter_kernel, owners),
        out_shape=(
            jax.ShapeDtypeStruct((bands_dev, rows_dev), bf16),
            jax.ShapeDtypeStruct((cap, owners * width), bf16),
        ),
        in_specs=[vmem, vmem, smem, smem, smem, vmem],
        out_specs=(vmem, vmem),
        scratch_shapes=[
            pltpu.VMEM((cap, bands_all), bf16),
            pltpu.VMEM((owners, bands_all, width), bf16),
            pltpu.VMEM((2, 2 * rows_dev, rows_dev), bf16),
            pltpu.VMEM((2, bands_dev // 2, 2 * rows_dev), bf16),
            pltpu.VMEM((bands_dev, rows_dev), bf16),
            pltpu.VMEM((bands_dev // 2, rows_dev), bf16),
            pltpu.VMEM((owners, cap, bands_dev), bf16),
            pltpu.VMEM((owners, cap, bands_dev), bf16),
            dma,
            dma,
            dma((4,)),
            dma((4,)),
            dma((4,)),
            dma((4,)),
            dma,
            dma,
            dma((owners,)),
            dma((owners,)),
            dma((2, hops)),
            dma((2, hops)),
            dma((2, hops)),
            dma((2, hops)),
            dma,
            dma,
        ],
        compiler_params=pltpu.CompilerParams(
            collective_id=0, has_side_effects=True, vmem_limit_bytes=40 * 1024 * 1024
        ),
        cost_estimate=pl.CostEstimate(
            flops=16 * bands_dev * 2 * rows_dev * rows_dev,
            bytes_accessed=200_000_000,
            transcendentals=0,
        ),
    )(start_bands, hamiltonian, neighbours, basis_count, owner_rows, rotation)


def solution(mesh):
    pair = mesh.shape["elem"] == 2 and mesh.shape["band"] % 4 == 0
    placed = (
        P("band", "elem"),
        P("elem", None, None, None),
        P("elem", None),
        P("elem"),
        P(),
        P(None, "band"),
    )
    return jax.shard_map(
        per_device_pair if pair else per_device,
        mesh=mesh,
        in_specs=placed,
        out_specs=(P("band", "elem"), P(("elem", "band"), None)),
        check_vma=False,
    )
```

```python
import functools

import jax
import jax.numpy as jnp
from jax import lax
from jax.experimental import pallas as pl
from jax.experimental.pallas import tpu as pltpu
from jax.sharding import PartitionSpec as P

DEGREE = 8


def padded_2(block, sides, width):
    for axis, dim in sides:
        count = lax.axis_size(axis)
        forward = [(i, i + 1) for i in range(count - 1)]
        forward.append((count - 1, 0))
        backward = [(target, source) for source, target in forward]
        low = lax.ppermute(
            lax.slice_in_dim(block, block.shape[dim] - width, None, axis=dim), axis, forward
        )
        high = lax.ppermute(lax.slice_in_dim(block, 0, width, axis=dim), axis, backward)
        block = jnp.concatenate([low, block, high], axis=dim)
    return block


def per_device(start_bands, hamiltonian, neighbours, basis_count, owner_rows, rotation):
    bands_dev, rows_dev = start_bands.shape
    elem_count = hamiltonian.shape[0]
    basis_max = hamiltonian.shape[2]
    planes_dev = elem_count // 4
    basis_ids = lax.broadcasted_iota(jnp.int32, (elem_count, basis_max), 1)
    row_mask = (basis_ids < basis_count[:, None]).astype(jnp.float32).reshape(rows_dev)
    partner_pick = (neighbours[:, :, None] == jnp.arange(4, dtype=jnp.int32)[None, None, :]).astype(
        jnp.bfloat16
    )
    partner_pick = partner_pick.reshape(planes_dev, 4, 6, 4)
    weights = hamiltonian.reshape(elem_count, 7 * basis_max, basis_max)

    def apply_ham(state):
        plane_slab = state.reshape(bands_dev, planes_dev, 4 * basis_max)
        extended = padded_2(plane_slab, (("elem", 1),), 1)
        extended = extended.reshape(bands_dev, planes_dev + 2, 4, basis_max)
        plane_below = extended[:, :planes_dev]
        plane_mid = extended[:, 1 : planes_dev + 1]
        plane_above = extended[:, 2:]
        inplane = jnp.einsum(
            "pism,bpmk->bpisk",
            partner_pick[:, :, :4],
            plane_mid,
            preferred_element_type=jnp.float32,
        ).astype(jnp.bfloat16)
        lower = jnp.einsum(
            "pim,bpmk->bpik", partner_pick[:, :, 4], plane_below, preferred_element_type=jnp.float32
        ).astype(jnp.bfloat16)
        upper = jnp.einsum(
            "pim,bpmk->bpik", partner_pick[:, :, 5], plane_above, preferred_element_type=jnp.float32
        ).astype(jnp.bfloat16)
        sources = jnp.concatenate(
            [plane_mid[:, :, :, None], inplane, lower[:, :, :, None], upper[:, :, :, None]], axis=3
        )
        sources = sources.reshape(bands_dev, elem_count, 7 * basis_max)
        product = jnp.einsum("bej,ejl->bel", sources, weights, preferred_element_type=jnp.float32)
        return product.reshape(bands_dev, rows_dev) * row_mask

    earlier = (start_bands.astype(jnp.float32) * row_mask).astype(jnp.bfloat16)
    current = (0.5 * apply_ham(earlier)).astype(jnp.bfloat16)
    for repeat in range(DEGREE - 1):
        following = (apply_ham(current) - earlier.astype(jnp.float32)).astype(jnp.bfloat16)
        earlier = current
        current = following
    owners = lax.axis_size("band")
    slot_cap = 3 * rows_dev // owners
    before = jnp.arange(owners)[None, :] < jnp.arange(owners)[:, None]
    row_starts = jnp.sum(jnp.where(before, owner_rows[None, :], 0), axis=1)
    slot_keep = jnp.arange(slot_cap, dtype=jnp.int32)[None, :] < owner_rows[:, None]
    padded = jnp.concatenate([current, jnp.zeros((bands_dev, slot_cap), jnp.bfloat16)], axis=1)
    pieces = jax.vmap(lambda offset: lax.dynamic_slice_in_dim(padded, offset, slot_cap, 1))(
        row_starts
    )
    owned_rows = lax.all_to_all(
        jnp.where(slot_keep[:, None, :], pieces, jnp.zeros((), jnp.bfloat16)),
        "band",
        split_axis=0,
        concat_axis=1,
        tiled=True,
    ).reshape(-1, slot_cap)
    rotated = lax.dot_general(
        owned_rows,
        lax.all_gather(rotation, "band", axis=1, tiled=True),
        (((0,), (0,)), ((), ())),
        preferred_element_type=jnp.float32,
    ).astype(jnp.bfloat16)
    return (current, rotated)


def filter_kernel(
    owners,
    start_ref,
    ham_ref,
    nb_ref,
    count_ref,
    owner_ref,
    rotation_ref,
    filtered_ref,
    rotated_ref,
    owned_ref,
    columns,
    amat,
    bands,
    masked,
    swapped,
    pieces,
    arrived,
    band_send,
    band_recv,
    strip_send,
    strip_recv,
    core_send,
    core_recv,
    back_send,
    back_recv,
    piece_send,
    piece_recv,
    ring_send,
    ring_recv,
    share_send,
    share_recv,
    mine_send,
    mine_recv,
):
    e = lax.axis_index("elem")
    b = lax.axis_index("band")
    o = 1 - e
    core = lax.rem(b, 2)
    sib = b + 1 - 2 * core
    count, rows = start_ref.shape
    half = count // 2
    nb = ham_ref.shape[2]
    cap = owned_ref.shape[0]

    barrier = pltpu.get_barrier_semaphore()
    pl.semaphore_signal(barrier, inc=1, device_id={"elem": o}, device_id_type=pl.DeviceIdType.MESH)

    def greet(d, carry):
        j = lax.rem(b + d, owners)
        pl.semaphore_signal(
            barrier, inc=1, device_id={"band": j}, device_id_type=pl.DeviceIdType.MESH
        )
        return carry

    lax.fori_loop(1, owners, greet, 0)
    pl.semaphore_wait(barrier, owners)

    chips = owners // 2
    tall = chips // 2
    chip = b // 2
    layer = chip // 2
    place = jnp.where(lax.rem(chip, 2) == 0, layer, chips - 1 - layer)
    depth = rotation_ref.shape[0] // 2

    def member(position, which):
        position = lax.rem(position + 2 * chips, chips)
        near = 4 * position
        far = 4 * (chips - 1 - position) + 2
        return jnp.where(position < tall, near, far) + which

    def part(chunk, way):
        return columns.at[chunk, pl.ds(way * depth, depth)]

    def ring_copy(step, way, chunk):
        return pltpu.make_async_remote_copy(
            src_ref=part(chunk, way),
            dst_ref=part(chunk, way),
            send_sem=ring_send.at[way, step],
            recv_sem=ring_recv.at[way, step],
            device_id={"band": member(place + 1 - 2 * way, core)},
            device_id_type=pl.DeviceIdType.MESH,
        )

    def sent_chunk(step, way, which):
        return member(place - step + 2 * step * way, which)

    def share_copy(step, way, which):
        chunk = sent_chunk(step + 1, way, which)
        return pltpu.make_async_remote_copy(
            src_ref=part(chunk, way),
            dst_ref=part(chunk, way),
            send_sem=share_send.at[way, step],
            recv_sem=share_recv.at[way, step],
            device_id={"band": sib},
            device_id_type=pl.DeviceIdType.MESH,
        )

    def mine_copy(chunk):
        return pltpu.make_async_remote_copy(
            src_ref=columns.at[chunk],
            dst_ref=columns.at[chunk],
            send_sem=mine_send,
            recv_sem=mine_recv,
            device_id={"band": sib},
            device_id_type=pl.DeviceIdType.MESH,
        )

    def ring(step):
        for way in range(2):
            if step > 0:
                ring_copy(step - 1, way, sent_chunk(step, way, core)).wait_recv()
            if step < chips - 1:
                ring_copy(step, way, sent_chunk(step, way, core)).start()
            if step > 0:
                share_copy(step - 1, way, core).start()

    columns[b] = rotation_ref[...]
    ring(0)
    mine_copy(b).start()

    lane = lax.broadcasted_iota(jnp.int32, (1, rows), 1)
    keep = jnp.zeros((1, rows), jnp.float32)
    for i in range(4):
        inside = (lane >= nb * i) & (lane < nb * i + count_ref[i])
        keep = jnp.where(inside, 1.0, keep)
    masked[...] = (start_ref[...].astype(jnp.float32) * keep).astype(jnp.bfloat16)
    own_cols = pl.ds(pl.multiple_of(rows * e, 128), rows)
    other_cols = pl.ds(pl.multiple_of(rows * o, 128), rows)
    own_half = pl.ds(pl.multiple_of(half * e, 16), half)
    other_half = pl.ds(pl.multiple_of(half * o, 16), half)
    band_copy = pltpu.make_async_remote_copy(
        src_ref=masked.at[other_half],
        dst_ref=bands.at[0, :, own_cols],
        send_sem=band_send,
        recv_sem=band_recv,
        device_id={"elem": o},
        device_id_type=pl.DeviceIdType.MESH,
    )
    band_copy.start()
    bands[0, :, own_cols] = masked[own_half, :]

    def strip_rows(step, side):
        t = 4 * side + step
        return pl.ds(pl.multiple_of(t * nb, 16), nb)

    def build(step, side):
        t = 4 * side + step
        parts = []
        for i in range(4):
            total = jnp.where(t == 4 * e + i, 1.0, 0.0) * ham_ref[i, 0].astype(jnp.float32)
            for j in range(1, 7):
                plane = e if j < 5 else o
                pick = jnp.where(nb_ref[i, j - 1] + 4 * plane == t, 1.0, 0.0)
                total = total + pick * ham_ref[i, j].astype(jnp.float32)
            parts.append(total)
        strip = jnp.concatenate(parts, axis=1) * keep
        amat[e, strip_rows(step, side), :] = strip.astype(jnp.bfloat16)

    def to_partner(step):
        where = strip_rows(step, core)
        return pltpu.make_async_remote_copy(
            src_ref=amat.at[e, where],
            dst_ref=amat.at[e, where],
            send_sem=strip_send.at[step],
            recv_sem=strip_recv.at[step],
            device_id={"elem": o},
            device_id_type=pl.DeviceIdType.MESH,
        )

    def from_partner(step):
        where = strip_rows(step, core)
        return pltpu.make_async_remote_copy(
            src_ref=amat.at[o, where],
            dst_ref=amat.at[o, where],
            send_sem=strip_send.at[step],
            recv_sem=strip_recv.at[step],
            device_id={"elem": o},
            device_id_type=pl.DeviceIdType.MESH,
        )

    def to_sibling(step, side):
        where = strip_rows(step, side)
        return pltpu.make_async_remote_copy(
            src_ref=amat.at[o, where],
            dst_ref=amat.at[o, where],
            send_sem=core_send.at[step],
            recv_sem=core_recv.at[step],
            device_id={"band": sib},
            device_id_type=pl.DeviceIdType.MESH,
        )

    def first_half(step, carry):
        build(step, core)
        to_partner(step).start()
        return carry

    def second_half(step, carry):
        build(step, 1 - core)
        return carry

    def forward(step, carry):
        from_partner(step).wait_recv()
        to_sibling(step, core).start()
        return carry

    def collect(step, carry):
        to_sibling(step, 1 - core).wait_recv()
        to_sibling(step, core).wait_send()
        to_partner(step).wait_send()
        return carry

    lax.fori_loop(0, 4, first_half, 0)
    lax.fori_loop(0, 4, second_half, 0)
    early = max(chips - 3, 0)
    for step in range(4):
        if step + 1 <= early:
            ring(step + 1)
        forward(step, 0)
    for step in range(5, early + 1):
        ring(step)
    lax.fori_loop(0, 4, collect, 0)
    band_copy.wait_send()
    pltpu.make_async_remote_copy(
        src_ref=masked.at[other_half],
        dst_ref=bands.at[0, :, other_cols],
        send_sem=band_send,
        recv_sem=band_recv,
        device_id={"elem": o},
        device_id_type=pl.DeviceIdType.MESH,
    ).wait_recv()

    wide = 256 if rows % 256 == 0 else rows

    def advance(now, later, first):
        for p in range(2):
            for c in range(rows // wide):
                product = jnp.dot(
                    bands[now],
                    amat[p, :, c * wide : (c + 1) * wide],
                    preferred_element_type=jnp.float32,
                )
                cols = slice(p * rows + c * wide, p * rows + (c + 1) * wide)
                if first:
                    product = 0.5 * product
                else:
                    product = product - bands[later, :, cols].astype(jnp.float32)
                bands[later, :, cols] = product.astype(jnp.bfloat16)

    advance(0, 1, True)

    def two_steps(k, carry):
        advance(1, 0, False)
        advance(0, 1, False)
        return carry

    split = (DEGREE - 2) // 4
    lax.fori_loop(0, split, two_steps, 0)
    for step in range(early + 1, chips - 1):
        ring(step)
    lax.fori_loop(split, (DEGREE - 2) // 2, two_steps, 0)
    advance(1, 0, False)

    back = pltpu.make_async_remote_copy(
        src_ref=bands.at[0, :, other_cols],
        dst_ref=swapped,
        send_sem=back_send,
        recv_sem=back_recv,
        device_id={"elem": o},
        device_id_type=pl.DeviceIdType.MESH,
    )
    back.start()
    masked[own_half, :] = bands[0, :, own_cols]
    back.wait()
    masked[other_half, :] = swapped[...]
    filtered_ref[...] = masked[...]

    lanes = lax.broadcasted_iota(jnp.int32, (cap, rows), 1)
    slots = lax.broadcasted_iota(jnp.int32, (cap, rows), 0)

    def piece(j):
        begin = jnp.int32(0)
        for i in range(owners):
            begin = begin + jnp.where(i < j, owner_ref[i], 0)
        chosen = (lanes == slots + begin) & (slots < owner_ref[j])
        pick = jnp.where(chosen, 1.0, 0.0).astype(jnp.bfloat16)
        return lax.dot_general(
            pick, masked[...], (((1,), (1,)), ((), ())), preferred_element_type=jnp.float32
        ).astype(jnp.bfloat16)

    def piece_copy(j, origin):
        return pltpu.make_async_remote_copy(
            src_ref=pieces.at[j],
            dst_ref=arrived.at[origin],
            send_sem=piece_send.at[j],
            recv_sem=piece_recv.at[origin],
            device_id={"band": j},
            device_id_type=pl.DeviceIdType.MESH,
        )

    def send(d, carry):
        j = lax.rem(b + d, owners)
        pieces[j] = piece(j)
        piece_copy(j, b).start()
        return carry

    lax.fori_loop(1, owners, send, 0)
    arrived[b] = piece(b)

    def receive(d, carry):
        j = lax.rem(b + d, owners)
        piece_copy(j, j).wait_recv()
        piece_copy(j, b).wait_send()
        return carry

    ring(chips - 1)
    lax.fori_loop(1, owners, receive, 0)
    for i in range(owners):
        owned_ref[:, i * count : (i + 1) * count] = arrived[i]
    mine_copy(b).wait_send()
    mine_copy(sib).wait_recv()
    for step in range(chips - 1):
        for way in range(2):
            ring_copy(step, way, sent_chunk(step, way, core)).wait_send()
            share_copy(step, way, core).wait_send()
            share_copy(step, way, 1 - core).wait_recv()
    width = rotation_ref.shape[1]

    def turn(pair, carry):
        wide = jnp.concatenate([columns[2 * pair], columns[2 * pair + 1]], axis=1)
        where = pl.ds(pl.multiple_of(pair * 2 * width, 128), 2 * width)
        rotated_ref[:, where] = jnp.dot(
            owned_ref[...], wide, preferred_element_type=jnp.float32
        ).astype(jnp.bfloat16)
        return carry

    lax.fori_loop(0, owners // 2, turn, 0)


def per_device_pair(start_bands, hamiltonian, neighbours, basis_count, owner_rows, rotation):
    bands_dev, rows_dev = start_bands.shape
    owners = lax.axis_size("band")
    cap = 3 * rows_dev // owners
    bands_all, width = rotation.shape
    hops = owners // 2 - 1
    vmem = pl.BlockSpec(memory_space=pltpu.VMEM)
    smem = pl.BlockSpec(memory_space=pltpu.SMEM)
    dma = pltpu.SemaphoreType.DMA
    bf16 = jnp.bfloat16
    return pl.pallas_call(
        functools.partial(filter_kernel, owners),
        out_shape=(
            jax.ShapeDtypeStruct((bands_dev, rows_dev), bf16),
            jax.ShapeDtypeStruct((cap, owners * width), bf16),
        ),
        in_specs=[vmem, vmem, smem, smem, smem, vmem],
        out_specs=(vmem, vmem),
        scratch_shapes=[
            pltpu.VMEM((cap, bands_all), bf16),
            pltpu.VMEM((owners, bands_all, width), bf16),
            pltpu.VMEM((2, 2 * rows_dev, rows_dev), bf16),
            pltpu.VMEM((2, bands_dev // 2, 2 * rows_dev), bf16),
            pltpu.VMEM((bands_dev, rows_dev), bf16),
            pltpu.VMEM((bands_dev // 2, rows_dev), bf16),
            pltpu.VMEM((owners, cap, bands_dev), bf16),
            pltpu.VMEM((owners, cap, bands_dev), bf16),
            dma,
            dma,
            dma((4,)),
            dma((4,)),
            dma((4,)),
            dma((4,)),
            dma,
            dma,
            dma((owners,)),
            dma((owners,)),
            dma((2, hops)),
            dma((2, hops)),
            dma((2, hops)),
            dma((2, hops)),
            dma,
            dma,
        ],
        compiler_params=pltpu.CompilerParams(
            collective_id=0, has_side_effects=True, vmem_limit_bytes=40 * 1024 * 1024
        ),
        cost_estimate=pl.CostEstimate(
            flops=16 * bands_dev * 2 * rows_dev * rows_dev,
            bytes_accessed=200_000_000,
            transcendentals=0,
        ),
    )(start_bands, hamiltonian, neighbours, basis_count, owner_rows, rotation)


def solution(mesh):
    pair = mesh.shape["elem"] == 2 and mesh.shape["band"] % 4 == 0
    placed = (
        P("band", "elem"),
        P("elem", None, None, None),
        P("elem", None),
        P("elem"),
        P(),
        P(None, "band"),
    )
    return jax.shard_map(
        per_device_pair if pair else per_device,
        mesh=mesh,
        in_specs=placed,
        out_specs=(P("band", "elem"), P(("elem", "band"), None)),
        check_vma=False,
    )
```
